512 devices in a mesh: ia: 8 (over y, core), wa: 8 (over z_lo), ao: 8 (over x, z_hi).
Axes of the slice: x: 4, y: 4, z: 16 (z_hi: 2, z_lo: 8; z = z_hi * 8 + z_lo), core: 2. Of those that a mesh axis runs over, the one named last changes fastest.
Arguments:
- tokens: bfloat16 [1024, 8192], P(('ia', 'ao'), 'wa'), may hold values from -6 to 6
- w_in: bfloat16 [8192, 16384], P('wa', ('ao', 'ia')), may hold values from -0.0625 to 0.0625
- w_out: bfloat16 [16384, 8192], P(('ao', 'ia'), 'wa'), may hold values from -0.046875 to 0.046875
- grad_out: bfloat16 [1024, 8192], P(('ia', 'ao'), 'wa'), may hold values from -6 to 6
Outputs:
- block_out: bfloat16 [1024, 8192], P(('ia', 'ao'), 'wa')
- grad_in: bfloat16 [1024, 8192], P(('ia', 'ao'), 'wa')
- grad_w_in: bfloat16 [8192, 16384], P('wa', ('ao', 'ia'))
- grad_w_out: bfloat16 [16384, 8192], P(('ao', 'ia'), 'wa')
The draws below stay inside these ranges and needn't reach their ends.
All inputs are finite; a program needn't handle non-finite values.
Results may differ from the reference program's by a relative error of at most 0.0049.
Values may be sent and summed in bfloat16 or wider, within the bound.
No kernel may reach another device: no remote copies, remote signals or barrier semaphores. Data moves between devices by JAX's collectives and lax.ppermute only.
A program may use at most 64 MiB of HBM per device.

```python
import jax
import jax.numpy as jnp
from jax import lax

D = 8192
FF = 16384
TOKENS = 1024


def block_scale(own_key, dims, shards, smallest, top_value):
    factor_of, own = 1.0, jax.random.fold_in(own_key, 6)
    for position, blocks in shards:
        draws = jnp.exp(jax.random.uniform(jax.random.fold_in(own, position), (blocks,), jnp.float32, smallest / len(shards), top_value / len(shards)))
        factor_of = factor_of * jnp.repeat(draws, dims[position] // blocks).reshape([-1 if axis == position else 1 for axis in range(len(dims))])
    return factor_of


def normal_values(own_key, extent, width, bound, pieces=(), dtype=jnp.bfloat16):
    drawn = jax.random.normal(own_key, extent, jnp.float32) * width
    if len(pieces) > 0:
        drawn = block_scale(own_key, extent, pieces, -0.22, 0.18) * drawn
    return jnp.clip(drawn, min=-bound, max=bound).astype(dtype)


def setup_inputs(seed: int = 0) -> dict:
    key_list = jax.random.split(jax.random.key(seed), 5)
    tokens = normal_values(key_list[0], (TOKENS, D), 1.0, 6.0, ((0, 64), (1, 8)))
    w_in = normal_values(key_list[1], (D, FF), D ** -0.5, 0.0625, ((0, 8), (1, 64)))
    w_out = normal_values(key_list[2], (FF, D), FF ** -0.5, 0.046875, ((0, 64), (1, 8)))
    grad_out = normal_values(key_list[3], (TOKENS, D), 1.0, 6.0, ((0, 64), (1, 8)))
    return {"tokens": tokens, "w_in": w_in, "w_out": w_out, "grad_out": grad_out}


inv_root_two = 0.7071067811865476
inv_root_tau = 0.3989422804014327


def gelu_pair(hidden):
    normal_cdf = 0.5 * (1.0 + lax.erf(hidden * inv_root_two))
    density = jnp.exp(-0.5 * hidden * hidden) * inv_root_tau
    return hidden * normal_cdf, normal_cdf + hidden * density


def reference(tokens, w_in, w_out, grad_out):
    hidden = jnp.dot(tokens, w_in, preferred_element_type=jnp.float32)
    act_full, slope = gelu_pair(hidden)
    act = act_full.astype(jnp.bfloat16)
    block_out = jnp.dot(act, w_out, preferred_element_type=jnp.float32).astype(jnp.bfloat16)
    grad_act = jnp.dot(grad_out, w_out.T, preferred_element_type=jnp.float32)
    grad_hidden = (grad_act * slope).astype(jnp.bfloat16)
    grad_in = jnp.dot(grad_hidden, w_in.T, preferred_element_type=jnp.float32).astype(jnp.bfloat16)
    grad_w_in = jnp.dot(tokens.T, grad_hidden, preferred_element_type=jnp.float32).astype(jnp.bfloat16)
    grad_w_out = jnp.dot(act.T, grad_out, preferred_element_type=jnp.float32).astype(jnp.bfloat16)
    return block_out, grad_in, grad_w_in, grad_w_out
```

```python
import jax
import jax.numpy as jnp
from jax import lax
from jax.sharding import Mesh, PartitionSpec as P

inv_root_two = 0.7071067811865476
inv_root_tau = 0.3989422804014327
bf16 = jnp.bfloat16
f32 = jnp.float32


def gelu_pair(hidden):
    normal_cdf = 0.5 * (1.0 + lax.erf(hidden * inv_root_two))
    density = jnp.exp(-0.5 * hidden * hidden) * inv_root_tau
    return (hidden * normal_cdf, normal_cdf + hidden * density)


def dot_nn(left, right):
    return jnp.dot(left, right, preferred_element_type=f32)


def dot_nt(left, right):
    return lax.dot_general(
        left, right, (((1,), (1,)), ((), ())), preferred_element_type=f32
    )


def dot_tn(left, right):
    return lax.dot_general(
        left, right, (((0,), (0,)), ((), ())), preferred_element_type=f32
    )


def swap(value, axis):
    return lax.ppermute(value, axis, [(0, 1), (1, 0)])


def exchange(value, axes):
    return lax.all_to_all(value, axes, 0, 0, tiled=True)


def gather_tokens(pair, which):
    copies = jnp.broadcast_to(pair[None], (16,) + pair.shape)
    return exchange(copies, ("y", "x")).reshape(512, pair.shape[1])


def sum_over_z(partial):
    parts = partial.astype(bf16).reshape(8, 64, 512)
    return jnp.sum(exchange(parts, "z").astype(f32), axis=0)


def gather_z(value):
    copies = jnp.broadcast_to(value[None], (8,) + value.shape)
    return exchange(copies, "z").reshape(512, 512)


def sum_tokens(partial):
    parts = partial.astype(bf16).reshape(16, 32, partial.shape[1])
    return jnp.sum(exchange(parts, ("y", "x")).astype(f32), axis=0)


def shards(tokens, w_in, w_out, grad_out):
    high = lax.axis_index("h") == 1
    w_in_b = swap(w_in, "c")
    w_out_b = swap(w_out, "c")
    both = jnp.stack([tokens, grad_out])
    other = swap(both, "h")
    low_rows = jnp.where(high, other, both)
    high_rows = jnp.where(high, both, other)
    pairs = jnp.concatenate([low_rows, high_rows], axis=1)
    x_half = gather_tokens(pairs[0], "x")
    dy_half = gather_tokens(pairs[1], "dy")
    x_other = swap(x_half, "c")
    dy_other = swap(dy_half, "c")

    hidden = sum_over_z(
        jnp.concatenate([dot_nn(x_half, w_in), dot_nn(x_half, w_in_b)], axis=1)
    )
    grad_act = sum_over_z(
        jnp.concatenate([dot_nt(dy_half, w_out), dot_nt(dy_half, w_out_b)], axis=1)
    )
    act_full, slope = gelu_pair(hidden)
    act = gather_z(act_full.astype(bf16))
    grad_hidden = gather_z((grad_act * slope).astype(bf16))

    out_part = sum_tokens(dot_nn(act[:, :256], w_out) + dot_nn(act[:, 256:], w_out_b))
    in_part = sum_tokens(
        dot_nt(grad_hidden[:, :256], w_in) + dot_nt(grad_hidden[:, 256:], w_in_b)
    )
    parts = jnp.stack([out_part, in_part])
    keep = jnp.where(high, parts[:, 16:], parts[:, :16])
    send = jnp.where(high, parts[:, :16], parts[:, 16:])
    outs = (keep + swap(send, "h")).astype(bf16)

    act_other = swap(act[:, 256:], "c")
    grad_other = swap(grad_hidden[:, 256:], "c")
    grad_w_in = dot_tn(x_half, grad_hidden[:, :256]) + dot_tn(x_other, grad_other)
    grad_w_out = dot_tn(act[:, :256], dy_half) + dot_tn(act_other, dy_other)
    return (outs[0], outs[1], grad_w_in.astype(bf16), grad_w_out.astype(bf16))


def solution(mesh):
    fine = Mesh(mesh.devices.reshape(4, 2, 8, 4, 2), ("y", "c", "z", "x", "h"))
    rows = P(("y", "c", "x", "h"), "z")
    w_in_spec = P("z", ("x", "h", "y", "c"))
    w_out_spec = P(("x", "h", "y", "c"), "z")
    return jax.shard_map(
        shards,
        mesh=fine,
        in_specs=(rows, w_in_spec, w_out_spec, rows),
        out_specs=(rows, rows, w_in_spec, w_out_spec),
        check_vma=False,
    )
```

```python
import jax
import jax.numpy as jnp
from jax import lax
from jax.sharding import Mesh, PartitionSpec as P

inv_root_two = 0.7071067811865476
inv_root_tau = 0.3989422804014327
bf16 = jnp.bfloat16
f32 = jnp.float32


def gelu_pair(hidden):
    normal_cdf = 0.5 * (1.0 + lax.erf(hidden * inv_root_two))
    density = jnp.exp(-0.5 * hidden * hidden) * inv_root_tau
    return (hidden * normal_cdf, normal_cdf + hidden * density)


def dot_nn(left, right):
    return jnp.dot(left, right, preferred_element_type=f32)


def dot_nt(left, right):
    return lax.dot_general(
        left, right, (((1,), (1,)), ((), ())), preferred_element_type=f32
    )


def dot_tn(left, right):
    return lax.dot_general(
        left, right, (((0,), (0,)), ((), ())), preferred_element_type=f32
    )


def swap(value, axis):
    return lax.ppermute(value, axis, [(0, 1), (1, 0)])


def flip(value, stride):
    return lax.ppermute(value, "z", [(i, i ^ stride) for i in range(8)])


def exchange(value):
    return lax.all_to_all(value, ("y", "x"), 0, 0, tiled=True)


def gather_rows(own):
    return exchange(jnp.broadcast_to(own[None], (16,) + own.shape))


def scatter_sum(first, second):
    width = first.shape[1]
    parts = jnp.stack(
        [first.astype(bf16).reshape(16, 16, width), second.astype(bf16).reshape(16, 16, width)],
        axis=1,
    )
    return jnp.sum(exchange(parts).astype(f32), axis=0)


def sum_quarter(partial):
    place = lax.axis_index("z")
    for stride in (1, 2):
        bit = (place // stride) % 2
        half = partial.shape[0] // 2
        send = lax.dynamic_slice_in_dim(partial, (1 - bit) * half, half).astype(bf16)
        keep = lax.dynamic_slice_in_dim(partial, bit * half, half)
        partial = keep + flip(send, stride).astype(f32)
    return partial + flip(partial.astype(bf16), 4).astype(f32)


def gather_quarters(value):
    place = lax.axis_index("z")
    for stride in (2, 1):
        upper = (place // stride) % 2 == 1
        other = flip(value, stride)
        value = jnp.concatenate(
            [jnp.where(upper, other, value), jnp.where(upper, value, other)]
        )
    return value


def shards(tokens, w_in, w_out, grad_out):
    n = tokens.shape[1]
    u = w_in.shape[1]
    own = jnp.stack([tokens, grad_out])
    near = gather_rows(own)
    far = gather_rows(swap(own, "h"))
    w_in_b = swap(w_in, "c")
    w_out_b = swap(w_out, "c")

    def front(rows):
        x = rows[:, 0].reshape(256, n)
        dy = rows[:, 1].reshape(256, n)
        partial = jnp.concatenate(
            [dot_nn(x, w_in), dot_nn(x, w_in_b), dot_nt(dy, w_out), dot_nt(dy, w_out_b)],
            axis=1,
        )
        total = sum_quarter(partial)
        act, slope = gelu_pair(total[:, : 2 * u])
        grad_hidden = total[:, 2 * u :] * slope
        return x, dy, jnp.concatenate([act.astype(bf16), grad_hidden.astype(bf16)], axis=1)

    def back(mid):
        out_part = dot_nn(mid[:, :u], w_out) + dot_nn(mid[:, u : 2 * u], w_out_b)
        in_part = dot_nt(mid[:, 2 * u : 3 * u], w_in) + dot_nt(mid[:, 3 * u :], w_in_b)
        return scatter_sum(out_part, in_part)

    x_near, dy_near, mid_near = front(near)
    x_far, dy_far, mid_far = front(far)
    mid_near = gather_quarters(mid_near)
    mid_far = gather_quarters(mid_far)
    far_sum = back(mid_far)
    near_sum = back(mid_near)
    outs = (near_sum + swap(far_sum, "h")).astype(bf16)

    def theirs(mid):
        return swap(jnp.concatenate([mid[:, u : 2 * u], mid[:, 3 * u :]], axis=1), "c")

    near_c, far_c = swap(near, "c"), swap(far, "c")
    x_all = jnp.concatenate(
        [x_near, x_far, near_c[:, 0].reshape(256, n), far_c[:, 0].reshape(256, n)]
    )
    dy_all = jnp.concatenate(
        [dy_near, dy_far, near_c[:, 1].reshape(256, n), far_c[:, 1].reshape(256, n)]
    )
    mids = (theirs(mid_near), theirs(mid_far))
    act_all = jnp.concatenate(
        [mid_near[:, :u], mid_far[:, :u]] + [m[:, :u] for m in mids]
    )
    grad_all = jnp.concatenate(
        [mid_near[:, 2 * u : 3 * u], mid_far[:, 2 * u : 3 * u]] + [m[:, u:] for m in mids]
    )
    grad_w_in = dot_tn(x_all, grad_all).astype(bf16)
    grad_w_out = dot_tn(act_all, dy_all).astype(bf16)
    return (outs[0], outs[1], grad_w_in, grad_w_out)


def solution(mesh):
    fine = Mesh(mesh.devices.reshape(4, 2, 8, 4, 2), ("y", "c", "z", "x", "h"))
    rows = P(("y", "c", "x", "h"), "z")
    w_in_spec = P("z", ("x", "h", "y", "c"))
    w_out_spec = P(("x", "h", "y", "c"), "z")
    return jax.shard_map(
        shards,
        mesh=fine,
        in_specs=(rows, w_in_spec, w_out_spec, rows),
        out_specs=(rows, rows, w_in_spec, w_out_spec),
        check_vma=False,
    )
```

```python
import jax
import jax.numpy as jnp
from jax import lax
from jax.experimental import pallas as pl
from jax.experimental.pallas import tpu as pltpu
from jax.sharding import Mesh, PartitionSpec as P

inv_root_two = 0.7071067811865476
inv_root_tau = 0.3989422804014327
bf16 = jnp.bfloat16
f32 = jnp.float32


def gelu_pair(hidden):
    normal_cdf = 0.5 * (1.0 + lax.erf(hidden * inv_root_two))
    density = jnp.exp(-0.5 * hidden * hidden) * inv_root_tau
    return (hidden * normal_cdf, normal_cdf + hidden * density)


def dot_nn(left, right):
    return jnp.dot(left, right, preferred_element_type=f32)


def dot_nt(left, right):
    return lax.dot_general(
        left, right, (((1,), (1,)), ((), ())), preferred_element_type=f32
    )


def dot_tn(left, right):
    return lax.dot_general(
        left, right, (((0,), (0,)), ((), ())), preferred_element_type=f32
    )


def swap(value, axis):
    return lax.ppermute(value, axis, [(0, 1), (1, 0)])


def exchange(value, axes=("y", "x")):
    return lax.all_to_all(value, axes, 0, 0, tiled=True)


def gather_rows(own):
    return exchange(jnp.broadcast_to(own[None], (16,) + own.shape))


def after(value, *others):
    return lax.optimization_barrier((value,) + others)[0]


def cross(value):
    return value + swap(value.astype(bf16), "zq").astype(f32)


def gather_four(value):
    copies = jnp.broadcast_to(value[None], (4,) + value.shape)
    return exchange(copies, ("zr",)).reshape(256, value.shape[1])


def halve(partial, stride, axis):
    bit = (lax.axis_index("zr") // stride) % 2
    send = lax.dynamic_index_in_dim(partial, 1 - bit, axis, keepdims=False)
    kept = lax.dynamic_index_in_dim(partial, bit, axis, keepdims=False)
    other = lax.ppermute(send.astype(bf16), "zr", [(i, i ^ stride) for i in range(4)])
    return kept + other.astype(f32)


def double(value, stride, axis):
    upper = (lax.axis_index("zr") // stride) % 2 == 1
    other = lax.ppermute(value, "zr", [(i, i ^ stride) for i in range(4)])
    return jnp.stack(
        [jnp.where(upper, other, value), jnp.where(upper, value, other)], axis=axis
    )


def front_kernel(rows, in_a, in_b, out_a, out_b, result):
    n, u = in_a.shape
    x = rows[:, 0].reshape(256, n)
    dy = rows[:, 1].reshape(256, n)
    for c, (w, v) in enumerate(((in_a, out_a), (in_b, out_b))):
        result[:, 2 * c * u : (2 * c + 1) * u] = dot_nn(x, w[...]).astype(result.dtype)
        result[:, (2 * c + 1) * u : (2 * c + 2) * u] = dot_nt(dy, v[...]).astype(
            result.dtype
        )


def back_kernel(mid, in_a, in_b, out_a, out_b, result):
    n, u = in_a.shape
    out_part = dot_nn(mid[:, :u], out_a[...]) + dot_nn(mid[:, 2 * u : 3 * u], out_b[...])
    result[:, 0] = out_part.astype(bf16).reshape(16, 16, n)
    in_part = dot_nt(mid[:, u : 2 * u], in_a[...]) + dot_nt(mid[:, 3 * u :], in_b[...])
    result[:, 1] = in_part.astype(bf16).reshape(16, 16, n)


def run(kernel, left, weights, shape, dtype):
    n, u = weights[0].shape
    result = jax.ShapeDtypeStruct(shape, dtype)
    return pl.pallas_call(
        kernel,
        out_shape=result,
        in_specs=[pl.BlockSpec(memory_space=pltpu.VMEM)] * 5,
        out_specs=pl.BlockSpec(memory_space=pltpu.VMEM),
        compiler_params=pltpu.CompilerParams(vmem_limit_bytes=32 * 1024 * 1024),
        cost_estimate=pl.CostEstimate(
            flops=2048 * n * u,
            bytes_accessed=2 * left.size + 8 * n * u + result.size * result.dtype.itemsize,
            transcendentals=0,
        ),
    )(left, *weights)


def both(*values):
    return lax.optimization_barrier(values)


def shards(tokens, w_in, w_out, grad_out):
    n = tokens.shape[1]
    u = w_in.shape[1]
    own = jnp.stack([tokens, grad_out])
    near = gather_rows(own)
    other_rows = swap(own, "h")
    weights = (w_in, swap(w_in, "c"), w_out, swap(w_out, "c"))

    def middle(total):
        parts = []
        for i in (0, 2 * u):
            act, slope = gelu_pair(total[:, i : i + u])
            grad_hidden = total[:, i + u : i + 2 * u] * slope
            parts += [act.astype(bf16), grad_hidden.astype(bf16)]
        return jnp.concatenate(parts, axis=1)

    def last(mid):
        return run(back_kernel, mid, weights, (16, 2, 16, n), bf16)

    def total_of(parts):
        return jnp.sum(exchange(parts).astype(f32), axis=0)

    far = gather_rows(after(other_rows, near))
    near_1 = run(front_kernel, near, weights, (256, 4 * u), f32)
    near_4 = halve(halve(near_1.reshape(2, 2, 64, 4 * u), 1, 1), 2, 0)
    far_1 = run(front_kernel, far, weights, (256, 4 * u), bf16)
    near_c = swap(near, "c")
    near_4, far_1 = both(near_4, far_1)
    far_4 = jnp.sum(
        exchange(far_1.reshape(4, 64, 4 * u), ("zr",)).astype(f32), axis=0
    )
    far_c = swap(far, "c")
    near_8, far_4, near_c = both(cross(near_4), far_4, near_c)
    far_8, mid_near, far_c = both(cross(far_4), double(middle(near_8), 2, 0), far_c)
    mid_far, mid_near = both(gather_four(middle(far_8)), double(mid_near, 1, 1))
    mid_near = mid_near.reshape(256, 4 * u)
    parts_far = last(mid_far)
    far_sum = total_of(parts_far)
    parts_near = last(mid_near)

    x_all = jnp.concatenate([r[:, 0].reshape(256, n) for r in (near, far, near_c, far_c)])
    dy_all = jnp.concatenate([r[:, 1].reshape(256, n) for r in (near, far, near_c, far_c)])
    far_sum, parts_near, mid_near, mid_far, x_all, dy_all = both(
        far_sum, parts_near, mid_near, mid_far, x_all, dy_all
    )
    mids = jnp.concatenate([mid_near, mid_far])
    theirs = swap(mids[:, 2 * u :], "c")
    act_all = jnp.concatenate([mids[:, :u], theirs[:, :u]])
    grad_all = jnp.concatenate([mids[:, u : 2 * u], theirs[:, u:]])
    grad_w_in = dot_tn(x_all, grad_all).astype(bf16)
    grad_w_out = dot_tn(act_all, dy_all).astype(bf16)
    near_sum = total_of(parts_near)
    outs = (near_sum + swap(far_sum, "h")).astype(bf16)
    return (outs[0], outs[1], grad_w_in, grad_w_out)


def solution(mesh):
    fine = Mesh(mesh.devices.reshape(4, 2, 2, 4, 4, 2), ("y", "c", "zq", "zr", "x", "h"))
    rows = P(("y", "c", "x", "h"), ("zq", "zr"))
    w_in_spec = P(("zq", "zr"), ("x", "h", "y", "c"))
    w_out_spec = P(("x", "h", "y", "c"), ("zq", "zr"))
    return jax.shard_map(
        shards,
        mesh=fine,
        in_specs=(rows, w_in_spec, w_out_spec, rows),
        out_specs=(rows, rows, w_in_spec, w_out_spec),
        check_vma=False,
    )
```

```python
import jax
import jax.numpy as jnp
from jax import lax
from jax.experimental import pallas as pl
from jax.experimental.pallas import tpu as pltpu
from jax.sharding import Mesh, PartitionSpec as P

inv_root_two = 0.7071067811865476
inv_root_tau = 0.3989422804014327
bf16 = jnp.bfloat16
f32 = jnp.float32


def gelu_pair(hidden):
    normal_cdf = 0.5 * (1.0 + lax.erf(hidden * inv_root_two))
    density = jnp.exp(-0.5 * hidden * hidden) * inv_root_tau
    return (hidden * normal_cdf, normal_cdf + hidden * density)


def dot_nn(left, right):
    return jnp.dot(left, right, preferred_element_type=f32)


def dot_nt(left, right):
    return lax.dot_general(
        left, right, (((1,), (1,)), ((), ())), preferred_element_type=f32
    )


def dot_tn(left, right):
    return lax.dot_general(
        left, right, (((0,), (0,)), ((), ())), preferred_element_type=f32
    )


def swap(value, axis):
    return lax.ppermute(value, axis, [(0, 1), (1, 0)])


def exchange(value, axes=("y", "x")):
    return lax.all_to_all(value, axes, 0, 0, tiled=True)


def gather_rows(own):
    return exchange(jnp.broadcast_to(own[None], (16,) + own.shape))


def after(value, *others):
    return lax.optimization_barrier((value,) + others)[0]


def cross(value):
    return value + swap(value.astype(bf16), "zq").astype(f32)


def gather_four(value):
    copies = jnp.broadcast_to(value[None], (4,) + value.shape)
    return exchange(copies, ("zr",)).reshape(256, value.shape[1])


def halve(partial, stride, axis):
    bit = (lax.axis_index("zr") // stride) % 2
    send = lax.dynamic_index_in_dim(partial, 1 - bit, axis, keepdims=False)
    kept = lax.dynamic_index_in_dim(partial, bit, axis, keepdims=False)
    other = lax.ppermute(send.astype(bf16), "zr", [(i, i ^ stride) for i in range(4)])
    return kept + other.astype(f32)


def double(value, stride, axis):
    upper = (lax.axis_index("zr") // stride) % 2 == 1
    other = lax.ppermute(value, "zr", [(i, i ^ stride) for i in range(4)])
    return jnp.stack(
        [jnp.where(upper, other, value), jnp.where(upper, value, other)], axis=axis
    )


def front_kernel(rows, in_a, in_b, out_a, out_b, result):
    n, u = in_a.shape
    x = rows[:, 0].reshape(256, n)
    dy = rows[:, 1].reshape(256, n)
    for c, (w, v) in enumerate(((in_a, out_a), (in_b, out_b))):
        result[:, 2 * c * u : (2 * c + 1) * u] = dot_nn(x, w[...]).astype(result.dtype)
        result[:, (2 * c + 1) * u : (2 * c + 2) * u] = dot_nt(dy, v[...]).astype(
            result.dtype
        )


def back_kernel(mid, in_a, in_b, out_a, out_b, result):
    n, u = in_a.shape
    out_part = dot_nn(mid[:, :u], out_a[...]) + dot_nn(mid[:, 2 * u : 3 * u], out_b[...])
    result[:, 0] = out_part.astype(bf16).reshape(16, 16, n)
    in_part = dot_nt(mid[:, u : 2 * u], in_a[...]) + dot_nt(mid[:, 3 * u :], in_b[...])
    result[:, 1] = in_part.astype(bf16).reshape(16, 16, n)


def run(kernel, left, weights, shape, dtype):
    n, u = weights[0].shape
    result = jax.ShapeDtypeStruct(shape, dtype)
    return pl.pallas_call(
        kernel,
        out_shape=result,
        in_specs=[pl.BlockSpec(memory_space=pltpu.VMEM)] * 5,
        out_specs=pl.BlockSpec(memory_space=pltpu.VMEM),
        compiler_params=pltpu.CompilerParams(vmem_limit_bytes=32 * 1024 * 1024),
        cost_estimate=pl.CostEstimate(
            flops=2048 * n * u,
            bytes_accessed=2 * left.size + 8 * n * u + result.size * result.dtype.itemsize,
            transcendentals=0,
        ),
    )(left, *weights)


def both(*values):
    return lax.optimization_barrier(values)


def shards(tokens, w_in, w_out, grad_out):
    n = tokens.shape[1]
    u = w_in.shape[1]
    own = jnp.stack([tokens, grad_out])
    near = gather_rows(own)
    other_rows = swap(own, "h")
    weights = (w_in, swap(w_in, "c"), w_out, swap(w_out, "c"))

    def middle(total):
        parts = []
        for i in (0, 2 * u):
            act, slope = gelu_pair(total[:, i : i + u])
            grad_hidden = total[:, i + u : i + 2 * u] * slope
            parts += [act.astype(bf16), grad_hidden.astype(bf16)]
        return jnp.concatenate(parts, axis=1)

    def last(mid):
        return run(back_kernel, mid, weights, (16, 2, 16, n), bf16)

    def total_of(parts):
        return jnp.sum(exchange(parts).astype(f32), axis=0)

    far = gather_rows(after(other_rows, near))
    near_1 = run(front_kernel, near, weights, (256, 4 * u), f32)
    near_4 = halve(halve(near_1.reshape(2, 2, 64, 4 * u), 1, 1), 2, 0)
    near_4, far = both(near_4, far)
    far_1 = run(front_kernel, far, weights, (256, 4 * u), bf16)
    near_c = swap(near, "c")
    far_4 = jnp.sum(
        exchange(far_1.reshape(4, 64, 4 * u), ("zr",)).astype(f32), axis=0
    )
    far_c = swap(far, "c")
    mid_near, far_4, near_c = both(double(middle(cross(near_4)), 2, 0), far_4, near_c)
    far_8, mid_near, far_c = both(cross(far_4), double(mid_near, 1, 1), far_c)
    mid_far = gather_four(middle(far_8))
    mid_near = mid_near.reshape(256, 4 * u)
    parts_far = last(mid_far)
    far_sum = total_of(parts_far)
    parts_near = last(mid_near)

    x_all = jnp.concatenate([r[:, 0].reshape(256, n) for r in (near, far, near_c, far_c)])
    dy_all = jnp.concatenate([r[:, 1].reshape(256, n) for r in (near, far, near_c, far_c)])
    theirs_near = swap(mid_near[:, 2 * u :], "c")
    late_far, x_all, dy_all = both(mid_far, x_all, dy_all)
    theirs_far = swap(late_far[:, 2 * u :], "c")
    mids = jnp.concatenate([mid_near[:, : 2 * u], mid_far[:, : 2 * u]])
    theirs = jnp.concatenate([theirs_near, theirs_far])
    far_sum, parts_near, mids, theirs = both(far_sum, parts_near, mids, theirs)
    act_all = jnp.concatenate([mids[:, :u], theirs[:, :u]])
    grad_all = jnp.concatenate([mids[:, u : 2 * u], theirs[:, u:]])
    grad_w_in = dot_tn(x_all, grad_all).astype(bf16)
    grad_w_out = dot_tn(act_all, dy_all).astype(bf16)
    near_sum = total_of(parts_near)
    outs = (near_sum + swap(far_sum.astype(bf16), "h").astype(f32)).astype(bf16)
    return (outs[0], outs[1], grad_w_in, grad_w_out)


def solution(mesh):
    fine = Mesh(mesh.devices.reshape(4, 2, 2, 4, 4, 2), ("y", "c", "zq", "zr", "x", "h"))
    rows = P(("y", "c", "x", "h"), ("zq", "zr"))
    w_in_spec = P(("zq", "zr"), ("x", "h", "y", "c"))
    w_out_spec = P(("x", "h", "y", "c"), ("zq", "zr"))
    return jax.shard_map(
        shards,
        mesh=fine,
        in_specs=(rows, w_in_spec, w_out_spec, rows),
        out_specs=(rows, rows, w_in_spec, w_out_spec),
        check_vma=False,
    )
```

```python
import jax
import jax.numpy as jnp
from jax import lax
from jax.experimental import pallas as pl
from jax.experimental.pallas import tpu as pltpu
from jax.sharding import Mesh, PartitionSpec as P

inv_root_two = 0.7071067811865476
inv_root_tau = 0.3989422804014327
bf16 = jnp.bfloat16
f32 = jnp.float32


def gelu_pair(hidden):
    normal_cdf = 0.5 * (1.0 + lax.erf(hidden * inv_root_two))
    density = jnp.exp(-0.5 * hidden * hidden) * inv_root_tau
    return (hidden * normal_cdf, normal_cdf + hidden * density)


def dot_nn(left, right):
    return jnp.dot(left, right, preferred_element_type=f32)


def dot_nt(left, right):
    return lax.dot_general(
        left, right, (((1,), (1,)), ((), ())), preferred_element_type=f32
    )


def dot_tn(left, right):
    return lax.dot_general(
        left, right, (((0,), (0,)), ((), ())), preferred_element_type=f32
    )


def swap(value, axis):
    return lax.ppermute(value, axis, [(0, 1), (1, 0)])


def exchange(value, axes=("y", "x")):
    return lax.all_to_all(value, axes, 0, 0, tiled=True)


def gather_rows(own):
    return exchange(jnp.broadcast_to(own[None], (16,) + own.shape))


def after(value, *others):
    return lax.optimization_barrier((value,) + others)[0]


def cross(value):
    return value + swap(value.astype(bf16), "zq").astype(f32)


def gather_four(value):
    copies = jnp.broadcast_to(value[None], (4,) + value.shape)
    return exchange(copies, ("zr",)).reshape(256, value.shape[1])


def halve(partial, stride, axis):
    bit = (lax.axis_index("zr") // stride) % 2
    send = lax.dynamic_index_in_dim(partial, 1 - bit, axis, keepdims=False)
    kept = lax.dynamic_index_in_dim(partial, bit, axis, keepdims=False)
    other = lax.ppermute(send.astype(bf16), "zr", [(i, i ^ stride) for i in range(4)])
    return kept + other.astype(f32)


def partner(value, stride):
    return lax.ppermute(value, "zr", [(i, i ^ stride) for i in range(4)])


def joined(value, other, stride, axis):
    upper = (lax.axis_index("zr") // stride) % 2 == 1
    return jnp.stack(
        [jnp.where(upper, other, value), jnp.where(upper, value, other)], axis=axis
    )


def double(value, stride, axis):
    return joined(value, partner(value, stride), stride, axis)


def front_kernel(rows, in_a, in_b, out_a, out_b, result):
    n, u = in_a.shape
    x = rows[:, 0].reshape(256, n)
    dy = rows[:, 1].reshape(256, n)
    for c, (w, v) in enumerate(((in_a, out_a), (in_b, out_b))):
        result[:, 2 * c * u : (2 * c + 1) * u] = dot_nn(x, w[...]).astype(result.dtype)
        result[:, (2 * c + 1) * u : (2 * c + 2) * u] = dot_nt(dy, v[...]).astype(
            result.dtype
        )


def back_kernel(mid, in_a, in_b, out_a, out_b, result):
    n, u = in_a.shape
    out_part = dot_nn(mid[:, :u], out_a[...]) + dot_nn(mid[:, 2 * u : 3 * u], out_b[...])
    result[:, 0] = out_part.astype(bf16).reshape(16, 16, n)
    in_part = dot_nt(mid[:, u : 2 * u], in_a[...]) + dot_nt(mid[:, 3 * u :], in_b[...])
    result[:, 1] = in_part.astype(bf16).reshape(16, 16, n)


def run(kernel, left, weights, shape, dtype):
    n, u = weights[0].shape
    result = jax.ShapeDtypeStruct(shape, dtype)
    return pl.pallas_call(
        kernel,
        out_shape=result,
        in_specs=[pl.BlockSpec(memory_space=pltpu.VMEM)] * 5,
        out_specs=pl.BlockSpec(memory_space=pltpu.VMEM),
        compiler_params=pltpu.CompilerParams(vmem_limit_bytes=32 * 1024 * 1024),
        cost_estimate=pl.CostEstimate(
            flops=2048 * n * u,
            bytes_accessed=2 * left.size + 8 * n * u + result.size * result.dtype.itemsize,
            transcendentals=0,
        ),
    )(left, *weights)


def both(*values):
    return lax.optimization_barrier(values)


def shards(tokens, w_in, w_out, grad_out):
    n = tokens.shape[1]
    u = w_in.shape[1]
    own = jnp.stack([tokens, grad_out])
    near = gather_rows(own)
    other_rows = swap(own, "h")
    weights = (w_in, swap(w_in, "c"), w_out, swap(w_out, "c"))

    def middle(total):
        parts = []
        for i in (0, 2 * u):
            act, slope = gelu_pair(total[:, i : i + u])
            grad_hidden = total[:, i + u : i + 2 * u] * slope
            parts += [act.astype(bf16), grad_hidden.astype(bf16)]
        return jnp.concatenate(parts, axis=1)

    def last(mid):
        return run(back_kernel, mid, weights, (16, 2, 16, n), bf16)

    def total_of(parts):
        return jnp.sum(exchange(parts).astype(f32), axis=0)

    far = gather_rows(after(other_rows, near))
    near_1 = run(front_kernel, near, weights, (256, 4 * u), f32)
    near_4 = halve(halve(near_1.reshape(2, 2, 64, 4 * u), 1, 1), 2, 0)
    near_4, far = both(near_4, far)
    far_1 = run(front_kernel, far, weights, (256, 4 * u), bf16)
    near_c = swap(near, "c")
    far_4 = jnp.sum(
        exchange(far_1.reshape(4, 64, 4 * u), ("zr",)).astype(f32), axis=0
    )
    far_c = swap(far, "c")
    near_8, far_4, near_c, far_c = both(cross(near_4), far_4, near_c, far_c)
    x_all = jnp.concatenate([r[:, 0].reshape(256, n) for r in (near, far, near_c, far_c)])
    dy_all = jnp.concatenate([r[:, 1].reshape(256, n) for r in (near, far, near_c, far_c)])
    mid_near = middle(near_8)
    far_8, mid_near, other, x_all, dy_all = both(
        cross(far_4), mid_near, partner(mid_near, 2), x_all, dy_all
    )
    mid_near = joined(mid_near, other, 2, 0)
    mid_far, mid_near = both(gather_four(middle(far_8)), double(mid_near, 1, 1))
    parts_far = last(mid_far)
    mid_near = mid_near.reshape(256, 4 * u)
    far_sum = total_of(parts_far)
    parts_near = last(mid_near)

    mids = jnp.concatenate([mid_near, mid_far])
    theirs = swap(mids[:, 2 * u :], "c")
    far_sum, parts_near, mids, theirs = both(far_sum, parts_near, mids, theirs)
    act_all = jnp.concatenate([mids[:, :u], theirs[:, :u]])
    grad_all = jnp.concatenate([mids[:, u : 2 * u], theirs[:, u:]])
    grad_w_in = dot_tn(x_all, grad_all).astype(bf16)
    grad_w_out = dot_tn(act_all, dy_all).astype(bf16)
    near_sum = total_of(parts_near)
    outs = (near_sum + swap(far_sum.astype(bf16), "h").astype(f32)).astype(bf16)
    return (outs[0], outs[1], grad_w_in, grad_w_out)


def solution(mesh):
    fine = Mesh(mesh.devices.reshape(4, 2, 2, 4, 4, 2), ("y", "c", "zq", "zr", "x", "h"))
    rows = P(("y", "c", "x", "h"), ("zq", "zr"))
    w_in_spec = P(("zq", "zr"), ("x", "h", "y", "c"))
    w_out_spec = P(("x", "h", "y", "c"), ("zq", "zr"))
    return jax.shard_map(
        shards,
        mesh=fine,
        in_specs=(rows, w_in_spec, w_out_spec, rows),
        out_specs=(rows, rows, w_in_spec, w_out_spec),
        check_vma=False,
    )
```

```python
import jax
import jax.numpy as jnp
from jax import lax
from jax.experimental import pallas as pl
from jax.experimental.pallas import tpu as pltpu
from jax.sharding import Mesh, PartitionSpec as P

inv_root_two = 0.7071067811865476
inv_root_tau = 0.3989422804014327
bf16 = jnp.bfloat16
f32 = jnp.float32


def gelu_pair(hidden):
    normal_cdf = 0.5 * (1.0 + lax.erf(hidden * inv_root_two))
    density = jnp.exp(-0.5 * hidden * hidden) * inv_root_tau
    return (hidden * normal_cdf, normal_cdf + hidden * density)


def dot_nn(left, right):
    return jnp.dot(left, right, preferred_element_type=f32)


def dot_nt(left, right):
    return lax.dot_general(
        left, right, (((1,), (1,)), ((), ())), preferred_element_type=f32
    )


def dot_tn(left, right):
    return lax.dot_general(
        left, right, (((0,), (0,)), ((), ())), preferred_element_type=f32
    )


def swap(value, axis):
    return lax.ppermute(value, axis, [(0, 1), (1, 0)])


def exchange(value, axes=("y", "x")):
    return lax.all_to_all(value, axes, 0, 0, tiled=True)


def gather_rows(own):
    return exchange(jnp.broadcast_to(own[None], (16,) + own.shape))


def after(value, *others):
    return lax.optimization_barrier((value,) + others)[0]


def cross(value):
    return value + swap(value.astype(bf16), "zq").astype(f32)


def gather_four(value):
    copies = jnp.broadcast_to(value[None], (4,) + value.shape)
    return exchange(copies, ("zr",)).reshape(256, value.shape[1])


def halve(partial, stride, axis):
    bit = (lax.axis_index("zr") // stride) % 2
    send = lax.dynamic_index_in_dim(partial, 1 - bit, axis, keepdims=False)
    kept = lax.dynamic_index_in_dim(partial, bit, axis, keepdims=False)
    other = lax.ppermute(send.astype(bf16), "zr", [(i, i ^ stride) for i in range(4)])
    return kept + other.astype(f32)


def partner(value, stride):
    return lax.ppermute(value, "zr", [(i, i ^ stride) for i in range(4)])


def joined(value, other, stride, axis):
    upper = (lax.axis_index("zr") // stride) % 2 == 1
    return jnp.stack(
        [jnp.where(upper, other, value), jnp.where(upper, value, other)], axis=axis
    )


def double(value, stride, axis):
    return joined(value, partner(value, stride), stride, axis)


def front_kernel(rows, in_a, in_b, out_a, out_b, result):
    n, u = in_a.shape
    x = rows[:, 0].reshape(256, n)
    dy = rows[:, 1].reshape(256, n)
    for c, (w, v) in enumerate(((in_a, out_a), (in_b, out_b))):
        result[:, 2 * c * u : (2 * c + 1) * u] = dot_nn(x, w[...]).astype(result.dtype)
        result[:, (2 * c + 1) * u : (2 * c + 2) * u] = dot_nt(dy, v[...]).astype(
            result.dtype
        )


def back_kernel(mid, in_a, in_b, out_a, out_b, result):
    n, u = in_a.shape
    out_part = dot_nn(mid[:, :u], out_a[...]) + dot_nn(mid[:, 2 * u : 3 * u], out_b[...])
    result[:, 0] = out_part.astype(bf16).reshape(16, 16, n)
    in_part = dot_nt(mid[:, u : 2 * u], in_a[...]) + dot_nt(mid[:, 3 * u :], in_b[...])
    result[:, 1] = in_part.astype(bf16).reshape(16, 16, n)


def run(kernel, left, weights, shape, dtype):
    n, u = weights[0].shape
    result = jax.ShapeDtypeStruct(shape, dtype)
    return pl.pallas_call(
        kernel,
        out_shape=result,
        in_specs=[pl.BlockSpec(memory_space=pltpu.VMEM)] * 5,
        out_specs=pl.BlockSpec(memory_space=pltpu.VMEM),
        compiler_params=pltpu.CompilerParams(vmem_limit_bytes=32 * 1024 * 1024),
        cost_estimate=pl.CostEstimate(
            flops=2048 * n * u,
            bytes_accessed=2 * left.size + 8 * n * u + result.size * result.dtype.itemsize,
            transcendentals=0,
        ),
    )(left, *weights)


def both(*values):
    return lax.optimization_barrier(values)


def shards(tokens, w_in, w_out, grad_out):
    n = tokens.shape[1]
    u = w_in.shape[1]
    own = jnp.stack([tokens, grad_out])
    near = gather_rows(own)
    other_rows = swap(own, "h")
    weights = (w_in, swap(w_in, "c"), w_out, swap(w_out, "c"))

    def middle(total):
        parts = []
        for i in (0, 2 * u):
            act, slope = gelu_pair(total[:, i : i + u])
            grad_hidden = total[:, i + u : i + 2 * u] * slope
            parts += [act.astype(bf16), grad_hidden.astype(bf16)]
        return jnp.concatenate(parts, axis=1)

    def last(mid):
        return run(back_kernel, mid, weights, (16, 2, 16, n), bf16)

    def total_of(parts):
        return jnp.sum(exchange(parts).astype(f32), axis=0)

    far = gather_rows(after(other_rows, near))
    near_1 = run(front_kernel, near, weights, (256, 4 * u), f32)
    near_4 = halve(halve(near_1.reshape(2, 2, 64, 4 * u), 1, 1), 2, 0)
    near_4, far = both(near_4, far)
    far_1 = run(front_kernel, far, weights, (256, 4 * u), bf16)
    near_c = swap(near, "c")
    far_4 = jnp.sum(
        exchange(far_1.reshape(4, 64, 4 * u), ("zr",)).astype(f32), axis=0
    )
    near_8, far_4, near_c = both(cross(near_4), far_4, near_c)
    mid_near = middle(near_8)
    far_8, mid_near, other, far = both(
        cross(far_4), mid_near, partner(mid_near, 2), far
    )
    far_c = swap(far, "c")
    mid_near = joined(mid_near, other, 2, 0)
    mid_far, mid_near, far_c = both(
        gather_four(middle(far_8)), double(mid_near, 1, 1), far_c
    )
    parts_far = last(mid_far)
    mid_near = mid_near.reshape(256, 4 * u)
    far_parts = exchange(parts_far)
    parts_near = last(mid_near)

    x_all = jnp.concatenate([r[:, 0].reshape(256, n) for r in (near, far, near_c, far_c)])
    dy_all = jnp.concatenate([r[:, 1].reshape(256, n) for r in (near, far, near_c, far_c)])
    mids = jnp.concatenate([mid_near, mid_far])
    theirs = swap(mids[:, 2 * u :], "c")
    far_parts, parts_near, mids, theirs, x_all, dy_all = both(
        far_parts, parts_near, mids, theirs, x_all, dy_all
    )
    far_sum = jnp.sum(far_parts.astype(f32), axis=0)
    act_all = jnp.concatenate([mids[:, :u], theirs[:, :u]])
    grad_all = jnp.concatenate([mids[:, u : 2 * u], theirs[:, u:]])
    grad_w_in = dot_tn(x_all, grad_all).astype(bf16)
    grad_w_out = dot_tn(act_all, dy_all).astype(bf16)
    near_sum = total_of(parts_near)
    outs = (near_sum + swap(far_sum.astype(bf16), "h").astype(f32)).astype(bf16)
    return (outs[0], outs[1], grad_w_in, grad_w_out)


def solution(mesh):
    fine = Mesh(mesh.devices.reshape(4, 2, 2, 4, 4, 2), ("y", "c", "zq", "zr", "x", "h"))
    rows = P(("y", "c", "x", "h"), ("zq", "zr"))
    w_in_spec = P(("zq", "zr"), ("x", "h", "y", "c"))
    w_out_spec = P(("x", "h", "y", "c"), ("zq", "zr"))
    return jax.shard_map(
        shards,
        mesh=fine,
        in_specs=(rows, w_in_spec, w_out_spec, rows),
        out_specs=(rows, rows, w_in_spec, w_out_spec),
        check_vma=False,
    )
```

```python
import jax
import jax.numpy as jnp
from jax import lax
from jax.experimental import pallas as pl
from jax.experimental.pallas import tpu as pltpu
from jax.sharding import Mesh, PartitionSpec as P

inv_root_two = 0.7071067811865476
inv_root_tau = 0.3989422804014327
bf16 = jnp.bfloat16
f32 = jnp.float32


def gelu_pair(hidden):
    normal_cdf = 0.5 * (1.0 + lax.erf(hidden * inv_root_two))
    density = jnp.exp(-0.5 * hidden * hidden) * inv_root_tau
    return (hidden * normal_cdf, normal_cdf + hidden * density)


def dot_nn(left, right):
    return jnp.dot(left, right, preferred_element_type=f32)


def dot_nt(left, right):
    return lax.dot_general(
        left, right, (((1,), (1,)), ((), ())), preferred_element_type=f32
    )


def dot_tn(left, right):
    return lax.dot_general(
        left, right, (((0,), (0,)), ((), ())), preferred_element_type=f32
    )


def swap(value, axis):
    return lax.ppermute(value, axis, [(0, 1), (1, 0)])


def exchange(value, axes=("y", "x")):
    return lax.all_to_all(value, axes, 0, 0, tiled=True)


def gather_rows(own):
    return exchange(jnp.broadcast_to(own[None], (16,) + own.shape))


def after(value, *others):
    return lax.optimization_barrier((value,) + others)[0]


def cross(value):
    return value + swap(value.astype(bf16), "zq").astype(f32)


def gather_four(value):
    copies = jnp.broadcast_to(value[None], (4,) + value.shape)
    return exchange(copies, ("zr",)).reshape(256, value.shape[1])


def halve(partial, stride, axis):
    bit = (lax.axis_index("zr") // stride) % 2
    send = lax.dynamic_index_in_dim(partial, 1 - bit, axis, keepdims=False)
    kept = lax.dynamic_index_in_dim(partial, bit, axis, keepdims=False)
    other = lax.ppermute(send.astype(bf16), "zr", [(i, i ^ stride) for i in range(4)])
    return kept + other.astype(f32)


def partner(value, stride):
    return lax.ppermute(value, "zr", [(i, i ^ stride) for i in range(4)])


def joined(value, other, stride, axis):
    upper = (lax.axis_index("zr") // stride) % 2 == 1
    return jnp.stack(
        [jnp.where(upper, other, value), jnp.where(upper, value, other)], axis=axis
    )


def double(value, stride, axis):
    return joined(value, partner(value, stride), stride, axis)


def front_kernel(rows, in_a, in_b, out_a, out_b, result):
    n, u = in_a.shape
    x = rows[:, 0].reshape(256, n)
    dy = rows[:, 1].reshape(256, n)
    for c, (w, v) in enumerate(((in_a, out_a), (in_b, out_b))):
        result[:, 2 * c * u : (2 * c + 1) * u] = dot_nn(x, w[...]).astype(result.dtype)
        result[:, (2 * c + 1) * u : (2 * c + 2) * u] = dot_nt(dy, v[...]).astype(
            result.dtype
        )


def back_kernel(mid, in_a, in_b, out_a, out_b, result):
    n, u = in_a.shape
    out_part = dot_nn(mid[:, :u], out_a[...]) + dot_nn(mid[:, 2 * u : 3 * u], out_b[...])
    result[:, 0] = out_part.astype(bf16).reshape(16, 16, n)
    in_part = dot_nt(mid[:, u : 2 * u], in_a[...]) + dot_nt(mid[:, 3 * u :], in_b[...])
    result[:, 1] = in_part.astype(bf16).reshape(16, 16, n)


def run(kernel, left, weights, shape, dtype):
    n, u = weights[0].shape
    result = jax.ShapeDtypeStruct(shape, dtype)
    return pl.pallas_call(
        kernel,
        out_shape=result,
        in_specs=[pl.BlockSpec(memory_space=pltpu.VMEM)] * 5,
        out_specs=pl.BlockSpec(memory_space=pltpu.VMEM),
        compiler_params=pltpu.CompilerParams(vmem_limit_bytes=32 * 1024 * 1024),
        cost_estimate=pl.CostEstimate(
            flops=2048 * n * u,
            bytes_accessed=2 * left.size + 8 * n * u + result.size * result.dtype.itemsize,
            transcendentals=0,
        ),
    )(left, *weights)


def both(*values):
    return lax.optimization_barrier(values)


def shards(tokens, w_in, w_out, grad_out):
    n = tokens.shape[1]
    u = w_in.shape[1]
    own = jnp.stack([tokens, grad_out])
    near = gather_rows(own)
    other_rows = swap(own, "h")
    weights = (w_in, swap(w_in, "c"), w_out, swap(w_out, "c"))

    def middle(total):
        parts = []
        for i in (0, 2 * u):
            act, slope = gelu_pair(total[:, i : i + u])
            grad_hidden = total[:, i + u : i + 2 * u] * slope
            parts += [act.astype(bf16), grad_hidden.astype(bf16)]
        return jnp.concatenate(parts, axis=1)

    def last(mid):
        return run(back_kernel, mid, weights, (16, 2, 16, n), bf16)

    def total_of(parts):
        return jnp.sum(exchange(parts).astype(f32), axis=0)

    far = gather_rows(after(other_rows, near))
    near_1 = run(front_kernel, near, weights, (256, 4 * u), f32)
    near_4 = halve(halve(near_1.reshape(2, 2, 64, 4 * u), 1, 1), 2, 0)
    near_4, far = both(near_4, far)
    far_1 = run(front_kernel, far, weights, (256, 4 * u), bf16)
    near_c = swap(near, "c")
    far_4 = jnp.sum(
        exchange(far_1.reshape(4, 64, 4 * u), ("zr",)).astype(f32), axis=0
    )
    far_c = swap(far, "c")
    near_8, far_4, near_c, far_c = both(cross(near_4), far_4, near_c, far_c)
    x_all = jnp.concatenate([r[:, 0].reshape(256, n) for r in (near, far, near_c, far_c)])
    dy_all = jnp.concatenate([r[:, 1].reshape(256, n) for r in (near, far, near_c, far_c)])
    mid_near = middle(near_8)
    far_8, mid_near, other, x_all, dy_all = both(
        cross(far_4), mid_near, partner(mid_near, 2), x_all, dy_all
    )
    mid_near = joined(mid_near, other, 2, 0)
    mid_far, mid_near = both(gather_four(middle(far_8)), double(mid_near, 1, 1))
    parts_far = last(mid_far)
    mid_near = mid_near.reshape(256, 4 * u)
    far_parts = exchange(parts_far)
    parts_near = last(mid_near)

    mids = jnp.concatenate([mid_near, mid_far])
    theirs = swap(mids[:, 2 * u :], "c")
    far_parts, parts_near, mids, theirs = both(far_parts, parts_near, mids, theirs)
    far_sum = jnp.sum(far_parts.astype(f32), axis=0)
    act_all = jnp.concatenate([mids[:, :u], theirs[:, :u]])
    grad_all = jnp.concatenate([mids[:, u : 2 * u], theirs[:, u:]])
    grad_w_in = dot_tn(x_all, grad_all).astype(bf16)
    grad_w_out = dot_tn(act_all, dy_all).astype(bf16)
    near_sum = total_of(parts_near)
    outs = (near_sum + swap(far_sum.astype(bf16), "h").astype(f32)).astype(bf16)
    return (outs[0], outs[1], grad_w_in, grad_w_out)


def solution(mesh):
    fine = Mesh(mesh.devices.reshape(4, 2, 2, 4, 4, 2), ("y", "c", "zq", "zr", "x", "h"))
    rows = P(("y", "c", "x", "h"), ("zq", "zr"))
    w_in_spec = P(("zq", "zr"), ("x", "h", "y", "c"))
    w_out_spec = P(("x", "h", "y", "c"), ("zq", "zr"))
    return jax.shard_map(
        shards,
        mesh=fine,
        in_specs=(rows, w_in_spec, w_out_spec, rows),
        out_specs=(rows, rows, w_in_spec, w_out_spec),
        check_vma=False,
    )
```
